512 devices in a mesh: seq: 64 (over y, z), kvh: 8 (over x, core).
Axes of the slice: x: 4, y: 4, z: 16, core: 2. Of those that a mesh axis runs over, the one named last changes fastest.
Arguments:
- queries: bfloat16 [192, 4, 8192], P('seq', None, 'kvh'), may hold values from -120 to 120
- new_keys: bfloat16 [192, 4, 1024], P('seq', None, 'kvh'), may hold values from -16 to 16
- new_values: bfloat16 [192, 4, 1024], P('seq', None, 'kvh'), may hold values from -6 to 6
- key_cache: bfloat16 [16, 8192, 1024], P(None, 'seq', 'kvh'), may hold values from -6 to 6
- value_cache: bfloat16 [16, 8192, 1024], P(None, 'seq', 'kvh'), may hold values from -6 to 6
- doc_ids: int32 [192], P('seq'), may hold values from 0 to 15
- prefix_len: int32 [192], P('seq'), may hold values from 4097 to 8192
- out_weight: bfloat16 [8192, 8192], P('kvh', 'seq'), may hold values from -0.25 to 0.25
Outputs:
- projected: bfloat16 [192, 4, 8192], P('kvh', None, 'seq')
The draws below stay inside these ranges and needn't reach their ends.
All inputs are finite; a program needn't handle non-finite values.
Results may differ from the reference program's by a relative error of at most 0.0046.
Values may be sent and summed in bfloat16 or wider, within the bound.
A program may use at most 64 MiB of HBM per device.

```python
import math
import jax
import jax.numpy as jnp
import numpy as np
from jax import lax

QH = 64
KVH = 8
HD = 128
D = 8192
DOCS = 16
STEPS = 4
TOKB = 128
DOCLEN = 8192
ROWS = 192
N_SEQ = 64


def draw_key_cache(key, part):
    key = jax.random.fold_in(key, 11)
    full_shape = (DOCS, DOCLEN, KVH * HD)
    sample = jnp.clip(jax.random.normal(key, full_shape, jnp.float32), -6.0, 6.0)
    return sample.astype(jnp.bfloat16)


def draw_queries(key, part):
    key = jax.random.fold_in(key, 23)
    full_shape = (ROWS, STEPS, QH * HD)
    sample = jnp.clip(2.5 * jax.random.normal(key, full_shape, jnp.float32), -15.0, 15.0)
    return sample.astype(jnp.bfloat16)


def place_ends(array, own_key, low, high):
    index_at = [jax.random.randint(jax.random.fold_in(own_key, axis), (), 0, length) for axis, length in enumerate(array.shape)]
    longest = array.shape.index(max(array.shape))
    next_to = index_at[:longest] + [(index_at[longest] + 1) % array.shape[longest]] + index_at[longest + 1:]
    return array.at[tuple(index_at)].set(low).at[tuple(next_to)].set(high)


def block_scale(key, dims, cuts, low, high):
    factor_of, own = 1.0, jax.random.fold_in(key, 6)
    for axis_at, blocks in cuts:
        heights = jnp.exp(jax.random.uniform(jax.random.fold_in(own, axis_at), (blocks,), jnp.float32, low / len(cuts), high / len(cuts)))
        factor_of = factor_of * jnp.repeat(heights, dims[axis_at] // blocks).reshape([-1 if axis == axis_at else 1 for axis in range(len(dims))])
    return factor_of


def cumulative_ranks(amount, skew):
    portions = [(1 << 20) // math.isqrt(grade ** skew) + 1 for grade in range(1, amount + 1)]
    spread = 1 + sum(portions) // (1 << 30)
    return np.cumsum(np.array([max(1, weight // spread) for weight in portions]))


def ranked_ids(stream_key, dims, count, slope):
    table = cumulative_ranks(count, slope)
    lot = jax.random.randint(jax.random.fold_in(stream_key, 1), dims, 0, int(table[count - 1]))
    grade = jnp.searchsorted(jnp.asarray(table, jnp.int32), lot, side="right")
    return jax.random.permutation(jax.random.fold_in(stream_key, 2), count)[grade].astype(jnp.int32)


def normal_values(stream_key, shape, width, bound, cuts=(), kind=jnp.bfloat16):
    result = jax.random.normal(stream_key, shape, jnp.float32) * width
    if len(cuts) > 0:
        result = block_scale(stream_key, shape, cuts, -0.22, 0.18) * result
    return jnp.clip(result, min=-bound, max=bound).astype(kind)


def setup_inputs(seed: int = 0) -> dict:
    splits = jax.random.split(jax.random.key(seed), 9)
    return {
        "queries": draw_queries(jax.random.fold_in(splits[8], 71), 0),
        "new_keys": normal_values(splits[1], (ROWS, STEPS, KVH * HD), 4.0, 16.0, ((0, 64), (2, 8))),
        "new_values": normal_values(splits[2], (ROWS, STEPS, KVH * HD), 1.0, 6.0, ((0, 64), (2, 8))),
        "key_cache": draw_key_cache(jax.random.fold_in(splits[8], 71), 0),
        "value_cache": normal_values(splits[4], (DOCS, DOCLEN, KVH * HD), 1.0, 6.0, ((1, 64), (2, 8))),
        "doc_ids": place_ends(ranked_ids(splits[5], (ROWS,), DOCS, 2), jax.random.fold_in(splits[5], 3), 0, DOCS - 1).astype(jnp.int32),
        "prefix_len": place_ends(jax.random.randint(splits[6], (ROWS,), DOCLEN // 2 + 1, DOCLEN + 1), jax.random.fold_in(splits[6], 1), DOCLEN // 2 + 1, DOCLEN).astype(jnp.int32),
        "out_weight": normal_values(splits[7], (QH * HD, D), (HD * 4) ** -0.5, 0.25, ((0, 8), (1, 64))),
    }


masked_score = -1e+30

def block_partial(query_view, key_block, value_block, length_rows, offset):
    score_scale = 1.0 / math.sqrt(query_view.shape[-1])
    scores = jnp.einsum('rshgd,rthd->rshgt', query_view.astype(jnp.float32), key_block.astype(jnp.float32)) * score_scale
    places = offset + jnp.arange(key_block.shape[1], dtype=jnp.int32)
    visible = (places[None, :] < length_rows[:, None])[:, None, None, None, :]
    masked = jnp.where(visible, scores, masked_score)
    peak_score = lax.optimization_barrier(jnp.max(masked, axis=4))
    weights = jnp.where(visible, jnp.exp(masked - peak_score[..., None]), 0.0)
    weight_sum = lax.optimization_barrier(jnp.sum(weights, axis=4))
    rounded = weights.astype(jnp.bfloat16)
    mixture = jnp.einsum('rshgt,rthd->rshgd', rounded.astype(jnp.float32), value_block.astype(jnp.float32))
    return (peak_score, weight_sum, mixture)

def own_partial(query_view, key_view, value_view):
    score_scale = 1.0 / math.sqrt(query_view.shape[-1])
    scores = jnp.einsum('rshgd,rkhd->rshgk', query_view.astype(jnp.float32), key_view.astype(jnp.float32)) * score_scale
    step_count = query_view.shape[1]
    causal = jnp.arange(step_count, dtype=jnp.int32)[None, :] <= jnp.arange(step_count, dtype=jnp.int32)[:, None]
    visible = causal[None, :, None, None, :]
    masked = jnp.where(visible, scores, masked_score)
    peak_score = lax.optimization_barrier(jnp.max(masked, axis=4))
    weights = jnp.where(visible, jnp.exp(masked - peak_score[..., None]), 0.0)
    weight_sum = lax.optimization_barrier(jnp.sum(weights, axis=4))
    rounded = weights.astype(jnp.bfloat16)
    mixture = jnp.einsum('rshgk,rkhd->rshgd', rounded.astype(jnp.float32), value_view.astype(jnp.float32))
    return (peak_score, weight_sum, mixture)

def merge_pair(first, second):
    peak_first, sum_first, mix_first = first
    peak_second, sum_second, mix_second = second
    peak_top = jnp.maximum(peak_first, peak_second)
    factor_first = jnp.exp(peak_first - peak_top)
    factor_second = jnp.exp(peak_second - peak_top)
    weight_sum = sum_first * factor_first + sum_second * factor_second
    mixture = mix_first * factor_first[..., None] + mix_second * factor_second[..., None]
    return (peak_top, weight_sum, mixture)

def reference(queries, new_keys, new_values, key_cache, value_cache, doc_ids, prefix_len, out_weight):
    row_count, step_count, row_width = queries.shape
    heads_kv = key_cache.shape[2] // HD
    group_size = row_width // (heads_kv * HD)
    query_view = queries.reshape(row_count, step_count, heads_kv, group_size, HD)

    def scan_block(carry, block_index):
        offset = (block_index * TOKB).astype(jnp.int32)
        key_block = lax.dynamic_slice_in_dim(key_cache, offset, TOKB, 1)[doc_ids].reshape(row_count, TOKB, heads_kv, HD)
        value_block = lax.dynamic_slice_in_dim(value_cache, offset, TOKB, 1)[doc_ids].reshape(row_count, TOKB, heads_kv, HD)
        part_now = block_partial(query_view, key_block, value_block, prefix_len, offset)
        return (merge_pair(carry, part_now), None)
    start_peak = jnp.full((row_count, step_count, heads_kv, group_size), masked_score, jnp.float32)
    start_sum = jnp.zeros((row_count, step_count, heads_kv, group_size), jnp.float32)
    start_mix = jnp.zeros((row_count, step_count, heads_kv, group_size, HD), jnp.float32)
    prefix_state, _ = lax.scan(scan_block, (start_peak, start_sum, start_mix), jnp.arange(N_SEQ, dtype=jnp.int32))
    own_state = own_partial(query_view, new_keys.reshape(row_count, step_count, heads_kv, HD), new_values.reshape(row_count, step_count, heads_kv, HD))
    peak_end, sum_end, mix_end = merge_pair(prefix_state, own_state)
    attention = (mix_end / sum_end[..., None]).astype(jnp.bfloat16).reshape(row_count * step_count, row_width)
    projected = jnp.dot(attention, out_weight, preferred_element_type=jnp.float32)
    return projected.astype(jnp.bfloat16).reshape(row_count, step_count, out_weight.shape[1])
```

```python
import functools
import math

import jax
import jax.numpy as jnp
from jax import lax
from jax.experimental import pallas as pl
from jax.experimental.pallas import tpu as pltpu
from jax.sharding import PartitionSpec as P

HD = 128
STEPS = 4
GROUP = 8
MESH = pl.DeviceIdType.MESH
masked_score = -1e30


def kernel(
    ny, nz, nk,
    q_ref, nk_ref, nv_ref, doc_ref, len_ref, k_hbm, v_hbm, w_hbm,
    out_ref,
    kbuf, vbuf, wbuf, qf, qg, idg, ids_s, own_a, own_l,
    ya, yl, ys, yst, yr, yrt, zs, zst, zr, zrt, ag, fs, ms, part, er,
    load_sem, ids_sem, idy_send, idy_recv,
    a_send, a_recv, i_send, i_recv, ay_send, ay_recv,
    cm_send, cm_recv, cl_send, cl_recv, zm_send, zm_recv, zl_send, zl_recv,
    d_send, d_recv, dy_send, dy_recv, e_send, e_recv,
):
    seq, kv = lax.axis_index("seq"), lax.axis_index("kvh")
    y, z = lax.div(seq, nz), lax.rem(seq, nz)
    rows = q_ref.shape[0]
    vec = STEPS * GROUP
    pairs = rows * STEPS
    size = rows * vec
    steps = nz // 2
    tok = k_hbm.shape[1]
    scale = 1.0 / math.sqrt(HD)

    def at(yy, zz):
        return (lax.rem(yy + ny, ny) * nz + lax.rem(zz + nz, nz), kv)

    right, left = at(y, z + 1), at(y, z - 1)

    def peer(j):
        return at(y + j, z)

    def remote(src, dst, ssem, rsem, dev):
        return pltpu.make_async_remote_copy(
            src_ref=src, dst_ref=dst, send_sem=ssem, recv_sem=rsem,
            device_id=dev, device_id_type=MESH,
        )

    barrier = pltpu.get_barrier_semaphore()
    for j in range(1, ny):
        pl.semaphore_signal(barrier, inc=1, device_id=peer(j), device_id_type=MESH)
    for c in range(1, nz):
        pl.semaphore_signal(barrier, inc=1, device_id=at(y, z + c), device_id_type=MESH)
    for c in range(1, nk):
        pl.semaphore_signal(
            barrier, inc=1, device_id=(seq, lax.rem(kv + c, nk)), device_id_type=MESH
        )

    loads = [
        pltpu.make_async_copy(k_hbm, kbuf, load_sem.at[0]),
        pltpu.make_async_copy(v_hbm, vbuf, load_sem.at[1]),
        pltpu.make_async_copy(w_hbm, wbuf, load_sem.at[2]),
    ]
    for load in loads:
        load.start()

    for r in range(rows):
        for h in range(GROUP):
            qf[pl.ds(r * vec + h, STEPS, stride=GROUP), :] = q_ref[
                r, :, h * HD:(h + 1) * HD
            ].astype(jnp.float32)
    qg[0, 0] = qf[...].astype(jnp.bfloat16)
    lane1 = lax.broadcasted_iota(jnp.int32, (1, HD), 1)
    own_ids = jnp.zeros((1, HD), jnp.int32)
    for r in range(rows):
        own_ids = jnp.where(lane1 == r, doc_ref[r], own_ids)
        own_ids = jnp.where(lane1 == rows + r, len_ref[r], own_ids)
    idg[0, 0] = own_ids

    pl.semaphore_wait(barrier, (ny - 1) + (nz - 1) + (nk - 1))

    def q_right(i):
        return remote(
            qg.at[0, 2 * i], qg.at[0, 2 * i + 2], a_send.at[2 * i], a_recv.at[2 * i + 2], right
        )

    def q_left(i):
        return remote(
            qg.at[0, 2 * i - 1], qg.at[0, 2 * i + 1], a_send.at[2 * i - 1], a_recv.at[2 * i + 1], left
        )

    def q_first():
        return remote(qg.at[0, 0], qg.at[0, 1], a_send.at[nz - 1], a_recv.at[1], left)

    def id_right(i):
        return remote(idg.at[2 * i], idg.at[2 * i + 2], i_send.at[2 * i], i_recv.at[2 * i + 2], right)

    def id_left(i):
        return remote(
            idg.at[2 * i - 1], idg.at[2 * i + 1], i_send.at[2 * i - 1], i_recv.at[2 * i + 1], left
        )

    def id_first():
        return remote(idg.at[0], idg.at[1], i_send.at[nz - 1], i_recv.at[1], left)

    def id_peer(j):
        return remote(
            idg.at[0, 0], idg.at[0, ny - j], idy_send.at[j], idy_recv.at[ny - j], peer(j)
        )

    def q_peer(i, j):
        return remote(
            qg.at[0, pl.ds(2 * i, 2)], qg.at[ny - j, pl.ds(2 * i, 2)],
            ay_send.at[i, j], ay_recv.at[i, ny - j], peer(j),
        )

    def ids_local(i):
        return pltpu.make_async_copy(
            idg.at[pl.ds(2 * i, 2)], ids_s.at[pl.ds(2 * i, 2)], ids_sem.at[i]
        )

    q_right(0).start()
    q_first().start()
    for j in range(1, ny):
        id_peer(j).start()

    step_of = lax.broadcasted_iota(jnp.int32, (vec, 1), 0) // GROUP
    lane8 = lax.broadcasted_iota(jnp.int32, (GROUP, HD), 1)
    stats = jnp.full((GROUP, HD), masked_score, jnp.float32)
    for r in range(rows):
        q = qf[r * vec:(r + 1) * vec, :]
        keys = nk_ref[r].astype(jnp.float32)
        values = nv_ref[r].astype(jnp.float32)
        scores = []
        for t in range(STEPS):
            score = jnp.sum(q * keys[t:t + 1, :], axis=1, keepdims=True) * scale
            scores.append(jnp.where(step_of >= t, score, masked_score))
        peak = scores[0]
        for t in range(1, STEPS):
            peak = jnp.maximum(peak, scores[t])
        total = jnp.zeros((vec, 1), jnp.float32)
        mix = jnp.zeros((vec, HD), jnp.float32)
        for t in range(STEPS):
            weight = jnp.where(step_of >= t, jnp.exp(scores[t] - peak), 0.0)
            total = total + weight
            mix = mix + weight.astype(jnp.bfloat16).astype(jnp.float32) * values[t:t + 1, :]
        own_a[r * vec:(r + 1) * vec, :] = mix / total
        lse = peak + jnp.log(total)
        for s in range(STEPS):
            stats = jnp.where(
                lane8 == r * STEPS + s, lse[s * GROUP:(s + 1) * GROUP, :], stats
            )
    own_l[...] = stats

    for j in range(1, ny):
        id_peer(ny - j).wait_recv()
    id_right(0).start()
    id_first().start()
    for load in loads:
        load.wait()

    places = seq * tok + lax.broadcasted_iota(jnp.int32, (1, tok), 1)

    def attend(j, c, write):
        packed = jnp.full((GROUP, HD), masked_score, jnp.float32)
        for r in range(rows):
            doc = ids_s[c, j, 0, r]
            length = ids_s[c, j, 0, rows + r]
            q = qg[j, c, r * vec:(r + 1) * vec, :]
            scores = lax.dot_general(
                q, kbuf[doc], (((1,), (1,)), ((), ())), preferred_element_type=jnp.float32
            ) * scale
            visible = places < length
            scores = jnp.where(visible, scores, masked_score)
            peak = jnp.max(scores, axis=1, keepdims=True)
            weights = jnp.where(visible, jnp.exp(scores - peak), 0.0)
            total = jnp.sum(weights, axis=1, keepdims=True)
            mix = jnp.dot(
                weights.astype(jnp.bfloat16), vbuf[doc], preferred_element_type=jnp.float32
            )
            seen = total > 0.0
            safe = jnp.where(seen, total, 1.0)
            write(slice(r * vec, (r + 1) * vec), mix / safe)
            lse = jnp.where(seen, peak + jnp.log(safe), masked_score)
            for s in range(STEPS):
                packed = jnp.where(
                    lane8 == r * STEPS + s, lse[s * GROUP:(s + 1) * GROUP, :], packed
                )
        return packed

    def y_mix(i, j):
        return remote(
            ys.at[j - 1, pl.ds(2 * i, 2)], yr.at[ny - j - 1, pl.ds(2 * i, 2)],
            cm_send.at[i, j], cm_recv.at[i, ny - j], peer(j),
        )

    def y_lse(i, j):
        return remote(
            yst.at[j - 1, pl.ds(2 * i, 2)], yrt.at[ny - j - 1, pl.ds(2 * i, 2)],
            cl_send.at[i, j], cl_recv.at[i, ny - j], peer(j),
        )

    def z_dev(c):
        i = lax.div(c, 2)
        return at(y, jnp.where(lax.rem(c, 2) == 0, z - i, z + i + 1))

    def z_mix(c):
        return remote(zs.at[c], zr.at[c], zm_send.at[c], zm_recv.at[c], z_dev(c))

    def z_lse(c):
        return remote(zst.at[c], zrt.at[c], zl_send.at[c], zl_recv.at[c], z_dev(c))

    def merge(parts, lses):
        top = lses[0]
        for lse in lses[1:]:
            top = jnp.maximum(top, lse)
        terms = [jnp.exp(lse - top) for lse in lses]
        total = terms[0]
        for term in terms[1:]:
            total = total + term
        factors = [term / total for term in terms]

        def rows_at(k):
            result = None
            for load_part, factor in zip(parts, factors):
                wide = jnp.concatenate(
                    [
                        jnp.broadcast_to(factor[:, 2 * k:2 * k + 1], (GROUP, HD)),
                        jnp.broadcast_to(factor[:, 2 * k + 1:2 * k + 2], (GROUP, HD)),
                    ],
                    axis=0,
                )
                term = load_part(slice(16 * k, 16 * k + 16)).astype(jnp.float32) * wide
                result = term if result is None else result + term
            return result

        return rows_at, top + jnp.log(total)

    def stage_a(i):
        @pl.when(i > 0)
        def _():
            q_right(i - 1).wait_recv()
            id_right(i - 1).wait_recv()

            @pl.when(i < steps - 1)
            def _():
                q_right(i).start()
                id_right(i).start()

        @pl.when(i == 0)
        def _():
            q_first().wait_recv()
            id_first().wait_recv()

        @pl.when(i > 0)
        def _():
            q_left(i).wait_recv()
            id_left(i).wait_recv()

        @pl.when(i < steps - 1)
        def _():
            q_left(i + 1).start()
            id_left(i + 1).start()

        for j in range(1, ny):
            q_peer(i, j).start()
        ids_local(i).start()

    def stage_b(i):
        ids_local(i).wait()
        for j in range(1, ny):
            q_peer(i, ny - j).wait_recv()

        @pl.loop(0, 2)
        def _(cc):
            c = 2 * i + cc
            for j in range(ny):
                if j == 0:
                    def write(where, value):
                        ya[c, where, :] = value

                    yl[c] = attend(j, c, write)
                else:
                    def write(where, value, j=j):
                        ys[j - 1, c, where, :] = value.astype(jnp.bfloat16)

                    yst[j - 1, c] = attend(j, c, write)

        for j in range(1, ny):
            y_mix(i, j).start()
            y_lse(i, j).start()

    def stage_c(i):
        for j in range(1, ny):
            y_mix(i, ny - j).wait_recv()
            y_lse(i, ny - j).wait_recv()

        @pl.loop(0, 2)
        def _(cc):
            c = 2 * i + cc
            parts = [lambda where: ya[c, where, :]]
            lses = [yl[c]]
            for j in range(1, ny):
                parts.append(lambda where, j=j: yr[j - 1, c, where, :])
                lses.append(yrt[j - 1, c])
            rows_at, lse = merge(parts, lses)
            for k in range(size // 16):
                zs[c, 16 * k:16 * k + 16, :] = rows_at(k).astype(jnp.bfloat16)
            zst[c] = lse

            @pl.when(c > 0)
            def _():
                z_mix(c).start()
                z_lse(c).start()

    @pl.loop(0, steps + 2)
    def _(i):
        @pl.when(i < steps)
        def _():
            stage_a(i)

        @pl.when(jnp.logical_and(i >= 1, i < steps + 1))
        def _():
            stage_b(i - 1)

        @pl.when(i >= 2)
        def _():
            stage_c(i - 2)

    @pl.loop(1, nz)
    def _(c):
        z_mix(c).wait_recv()
        z_lse(c).wait_recv()

    parts = [lambda where: own_a[where, :], lambda where: zs[0, where, :]]
    lses = [own_l[...], zst[0]]
    for c in range(1, nz):
        parts.append(lambda where, c=c: zr[c, where, :])
        lses.append(zrt[c])
    rows_at, _ = merge(parts, lses)
    for k in range(size // 16):
        ag[0, 0, 16 * k:16 * k + 16, :] = rows_at(k).astype(jnp.bfloat16)

    def d_right(i):
        return remote(
            ag.at[0, 2 * i], ag.at[0, 2 * i + 2], d_send.at[2 * i], d_recv.at[2 * i + 2], right
        )

    def d_left(i):
        return remote(
            ag.at[0, 2 * i - 1], ag.at[0, 2 * i + 1], d_send.at[2 * i - 1], d_recv.at[2 * i + 1], left
        )

    def d_first():
        return remote(ag.at[0, 0], ag.at[0, 1], d_send.at[nz - 1], d_recv.at[1], left)

    def d_peer(i, j):
        return remote(
            ag.at[0, pl.ds(2 * i, 2)], ag.at[ny - j, pl.ds(2 * i, 2)],
            dy_send.at[i, j], dy_recv.at[i, ny - j], peer(j),
        )

    d_right(0).start()
    d_first().start()

    def gather(i):
        @pl.when(i > 0)
        def _():
            d_right(i - 1).wait_recv()

            @pl.when(i < steps - 1)
            def _():
                d_right(i).start()

        @pl.when(i == 0)
        def _():
            d_first().wait_recv()

        @pl.when(i > 0)
        def _():
            d_left(i).wait_recv()

        @pl.when(i < steps - 1)
        def _():
            d_left(i + 1).start()

        for j in range(1, ny):
            d_peer(i, j).start()

    def project(i):
        for j in range(1, ny):
            d_peer(i, ny - j).wait_recv()
        for cc in range(2):
            for j in range(ny):
                first = (cc * ny + j) * size
                fs[first:first + size, :] = ag[j, 2 * i + cc].astype(jnp.float32)
        total = None
        for h in range(GROUP):
            piece = fs[pl.ds(h, 2 * ny * pairs, stride=GROUP), :].astype(jnp.bfloat16)
            term = jnp.dot(
                piece, wbuf[h * HD:(h + 1) * HD, :], preferred_element_type=jnp.float32
            )
            total = term if total is None else total + term
        ms[...] = total
        for cc in range(2):
            column = lax.rem((z - i if cc == 0 else z + i + 1) + nz, nz)
            for j in range(ny):
                owner = lax.rem(y + j, ny) * nz + column
                first = (cc * ny + j) * pairs
                part[owner] = ms[first:first + pairs, :]

    @pl.loop(0, steps + 1)
    def _(i):
        @pl.when(i < steps)
        def _():
            gather(i)

        @pl.when(i >= 1)
        def _():
            project(i - 1)

    blocks = ny * nz // nk

    def e_copy(c):
        other = lax.rem(kv + c, nk)
        return remote(
            part.at[pl.ds(other * blocks, blocks)], er.at[nk - c],
            e_send.at[c], e_recv.at[nk - c], (seq, other),
        )

    for c in range(1, nk):
        e_copy(c).start()
    for c in range(1, nk):
        e_copy(nk - c).wait_recv()
    result = part[pl.ds(kv * blocks, blocks)]
    for c in range(1, nk):
        result = result + er[c]
    out_ref[...] = result.astype(out_ref.dtype)

    q_first().wait_send()
    id_first().wait_send()
    d_first().wait_send()

    @pl.loop(0, steps - 1)
    def _(i):
        q_right(i).wait_send()
        id_right(i).wait_send()
        d_right(i).wait_send()
        q_left(i + 1).wait_send()
        id_left(i + 1).wait_send()
        d_left(i + 1).wait_send()

    for j in range(1, ny):
        id_peer(j).wait_send()

    @pl.loop(0, steps)
    def _(i):
        for j in range(1, ny):
            q_peer(i, j).wait_send()
            y_mix(i, j).wait_send()
            y_lse(i, j).wait_send()
            d_peer(i, j).wait_send()

    @pl.loop(1, nz)
    def _(c):
        z_mix(c).wait_send()
        z_lse(c).wait_send()

    for c in range(1, nk):
        e_copy(c).wait_send()


def solution(mesh, ny=None):
    nseq, nk = mesh.shape["seq"], mesh.shape["kvh"]
    ny = 4 if ny is None else ny
    nz = nseq // ny
    steps = nz // 2

    def shards(queries, new_keys, new_values, key_cache, value_cache, doc_ids, prefix_len, out_weight):
        rows = queries.shape[0]
        size = rows * STEPS * GROUP
        pairs = rows * STEPS
        blocks = nseq // nk
        bf, f32 = jnp.bfloat16, jnp.float32
        vmem = pl.BlockSpec(memory_space=pltpu.VMEM)
        smem = pl.BlockSpec(memory_space=pltpu.SMEM)
        anyw = pl.BlockSpec(memory_space=pl.ANY)
        dma = pltpu.SemaphoreType.DMA
        result = pl.pallas_call(
            functools.partial(kernel, ny, nz, nk),
            out_shape=jax.ShapeDtypeStruct((blocks, pairs, HD), bf),
            in_specs=[vmem, vmem, vmem, smem, smem, anyw, anyw, anyw],
            out_specs=vmem,
            scratch_shapes=[
                pltpu.VMEM(key_cache.shape, bf),
                pltpu.VMEM(value_cache.shape, bf),
                pltpu.VMEM(out_weight.shape, bf),
                pltpu.VMEM((size, HD), f32),
                pltpu.VMEM((ny, nz, size, HD), bf),
                pltpu.VMEM((nz, ny, 1, HD), jnp.int32),
                pltpu.SMEM((nz, ny, 1, HD), jnp.int32),
                pltpu.VMEM((size, HD), f32),
                pltpu.VMEM((GROUP, HD), f32),
                pltpu.VMEM((nz, size, HD), f32),
                pltpu.VMEM((nz, GROUP, HD), f32),
                pltpu.VMEM((ny - 1, nz, size, HD), bf),
                pltpu.VMEM((ny - 1, nz, GROUP, HD), f32),
                pltpu.VMEM((ny - 1, nz, size, HD), bf),
                pltpu.VMEM((ny - 1, nz, GROUP, HD), f32),
                pltpu.VMEM((nz, size, HD), bf),
                pltpu.VMEM((nz, GROUP, HD), f32),
                pltpu.VMEM((nz, size, HD), bf),
                pltpu.VMEM((nz, GROUP, HD), f32),
                pltpu.VMEM((ny, nz, size, HD), bf),
                pltpu.VMEM((2 * ny * size, HD), f32),
                pltpu.VMEM((2 * ny * pairs, HD), f32),
                pltpu.VMEM((nseq, pairs, HD), f32),
                pltpu.VMEM((nk, blocks, pairs, HD), f32),
                dma((3,)), dma((steps,)), dma((ny,)), dma((ny,)),
                dma((nz,)), dma((nz,)), dma((nz,)), dma((nz,)),
                dma((steps, ny)), dma((steps, ny)),
                dma((steps, ny)), dma((steps, ny)), dma((steps, ny)), dma((steps, ny)),
                dma((nz,)), dma((nz,)), dma((nz,)), dma((nz,)),
                dma((nz,)), dma((nz,)), dma((steps, ny)), dma((steps, ny)),
                dma((nk,)), dma((nk,)),
            ],
            compiler_params=pltpu.CompilerParams(
                collective_id=0, has_side_effects=True, vmem_limit_bytes=40 * 1024 * 1024
            ),
        )(queries, new_keys, new_values, doc_ids, prefix_len, key_cache, value_cache, out_weight)
        return result.reshape(nseq * rows // nk, STEPS, HD)

    return jax.shard_map(
        shards,
        mesh=mesh,
        in_specs=(
            P("seq", None, "kvh"),
            P("seq", None, "kvh"),
            P("seq", None, "kvh"),
            P(None, "seq", "kvh"),
            P(None, "seq", "kvh"),
            P("seq"),
            P("seq"),
            P("kvh", "seq"),
        ),
        out_specs=P("kvh", None, "seq"),
        check_vma=False,
    )
```

```python
import functools
import math

import jax
import jax.numpy as jnp
from jax import lax
from jax.experimental import pallas as pl
from jax.experimental.pallas import tpu as pltpu
from jax.sharding import PartitionSpec as P

HD = 128
STEPS = 4
GROUP = 8
MESH = pl.DeviceIdType.MESH
masked_score = -1e30


def kernel(
    ny, nz, nk,
    q_hbm, nk_hbm, nv_hbm, doc_hbm, len_hbm, k_hbm, v_hbm, w_hbm,
    out_ref,
    q_ref, nk_ref, nv_ref, doc_ref, len_ref, kbuf, kt, vbuf, wbuf, qf, qg, idg, ids_s, own_a, own_l,
    ya, yl, ys, yst, yr, yrt, zs, zst, zr, zrt, ag, fs, ms, part, er,
    load_sem, ids_sem, iy_send, iy_recv,
    a_send, a_recv, i_send, i_recv, ay_send, ay_recv, ar_send, ar_recv,
    cm_send, cm_recv, cl_send, cl_recv, zm_send, zm_recv, zl_send, zl_recv,
    d_send, d_recv, dy_send, dy_recv, e_send, e_recv,
):
    seq, kv = lax.axis_index("seq"), lax.axis_index("kvh")
    y, z = lax.div(seq, nz), lax.rem(seq, nz)
    rows = q_ref.shape[0]
    vec = STEPS * GROUP
    pairs = rows * STEPS
    size = rows * vec
    steps = nz // 2
    tok = k_hbm.shape[1]
    scale = 1.0 / math.sqrt(HD)

    def at(yy, zz):
        return (lax.rem(yy + ny, ny) * nz + lax.rem(zz + nz, nz), kv)

    def peer(j):
        return at(y + j, z)

    def remote(src, dst, ssem, rsem, dev):
        return pltpu.make_async_remote_copy(
            src_ref=src, dst_ref=dst, send_sem=ssem, recv_sem=rsem,
            device_id=dev, device_id_type=MESH,
        )

    barrier = pltpu.get_barrier_semaphore()
    for j in range(1, ny):
        pl.semaphore_signal(barrier, inc=1, device_id=peer(j), device_id_type=MESH)
    for c in range(1, nz):
        pl.semaphore_signal(barrier, inc=1, device_id=at(y, z + c), device_id_type=MESH)
    for c in range(1, nk):
        pl.semaphore_signal(
            barrier, inc=1, device_id=(seq, lax.rem(kv + c, nk)), device_id_type=MESH
        )

    loads = [
        pltpu.make_async_copy(src, dst, load_sem.at[n])
        for n, (src, dst) in enumerate([
            (q_hbm, q_ref), (doc_hbm, doc_ref), (len_hbm, len_ref), (nk_hbm, nk_ref),
            (nv_hbm, nv_ref), (k_hbm, kbuf), (v_hbm, vbuf), (w_hbm, wbuf),
        ])
    ]
    for load in loads:
        load.start()
    for load in loads[:3]:
        load.wait()

    for r in range(rows):
        for h in range(GROUP):
            qf[pl.ds(r * vec + h, STEPS, stride=GROUP), :] = q_ref[
                r, :, h * HD:(h + 1) * HD
            ].astype(jnp.float32)
    qg[0, 0] = qf[...].astype(jnp.bfloat16)
    lane1 = lax.broadcasted_iota(jnp.int32, (1, HD), 1)
    own_ids = jnp.zeros((1, HD), jnp.int32)
    for r in range(rows):
        own_ids = jnp.where(lane1 == r, doc_ref[r], own_ids)
        own_ids = jnp.where(lane1 == rows + r, len_ref[r], own_ids)
    idg[0, 0] = own_ids

    pl.semaphore_wait(barrier, (ny - 1) + (nz - 1) + (nk - 1))

    def column(c):
        i = lax.div(c, 2)
        return jnp.where(lax.rem(c, 2) == 0, z - i, z + i + 1)

    def mirror(c):
        i = lax.div(c, 2)
        return at(y, jnp.where(lax.rem(c, 2) == 0, z + i, z - i - 1))

    def q_send(c):
        return remote(qg.at[0, 0], qg.at[0, c], a_send.at[c], a_recv.at[c], mirror(c))

    def id_send(c):
        return remote(idg.at[0, 0], idg.at[0, c], i_send.at[c], i_recv.at[c], mirror(c))

    def id_peer(i, j):
        return remote(
            idg.at[0, pl.ds(2 * i, 2)], idg.at[ny - j, pl.ds(2 * i, 2)],
            iy_send.at[i, j], iy_recv.at[i, ny - j], peer(j),
        )

    def q_peer(i, j):
        return remote(
            qg.at[0, pl.ds(2 * i, 2)], qg.at[ny - j, pl.ds(2 * i, 2)],
            ay_send.at[i, j], ay_recv.at[i, ny - j], peer(j),
        )

    def q_relay(i, j):
        c = 2 * i + (j - 1) // 2
        return remote(
            qg.at[ny - j, c], qg.at[2, c], ar_send.at[i, j], ar_recv.at[i, ny - j], peer(j)
        )

    def ids_local(i):
        return pltpu.make_async_copy(
            idg.at[:, pl.ds(2 * i, 2)], ids_s.at[:, pl.ds(2 * i, 2)], ids_sem.at[i]
        )

    for c in range(1, nz):
        id_send(c).start()
    for c in range(1, nz):
        q_send(c).start()

    lane8 = lax.broadcasted_iota(jnp.int32, (GROUP, HD), 1)

    def own_tokens():
        loads[3].wait()
        loads[4].wait()
        step_of = lax.broadcasted_iota(jnp.int32, (vec, 1), 0) // GROUP
        stats = jnp.full((GROUP, HD), masked_score, jnp.float32)
        for r in range(rows):
            q = qf[r * vec:(r + 1) * vec, :]
            keys = nk_ref[r].astype(jnp.float32)
            values = nv_ref[r].astype(jnp.float32)
            scores = []
            for t in range(STEPS):
                score = jnp.sum(q * keys[t:t + 1, :], axis=1, keepdims=True) * scale
                scores.append(jnp.where(step_of >= t, score, masked_score))
            peak = scores[0]
            for t in range(1, STEPS):
                peak = jnp.maximum(peak, scores[t])
            total = jnp.zeros((vec, 1), jnp.float32)
            mix = jnp.zeros((vec, HD), jnp.float32)
            for t in range(STEPS):
                weight = jnp.where(step_of >= t, jnp.exp(scores[t] - peak), 0.0)
                total = total + weight
                mix = mix + weight.astype(jnp.bfloat16).astype(jnp.float32) * values[t:t + 1, :]
            own_a[r * vec:(r + 1) * vec, :] = mix / total
            lse = peak + jnp.log(total)
            for s in range(STEPS):
                stats = jnp.where(
                    lane8 == r * STEPS + s, lse[s * GROUP:(s + 1) * GROUP, :], stats
                )
        own_l[...] = stats

    def ready():
        for load in loads[5:]:
            load.wait()

        for d in range(kbuf.shape[0]):
            kt[d] = kbuf[d].T

        yl[...] = jnp.full(yl.shape, masked_score, jnp.float32)
        yst[...] = jnp.full(yst.shape, masked_score, jnp.float32)

    places = seq * tok + lax.broadcasted_iota(jnp.int32, (1, tok), 1)

    def attend(jobs, half):
        scores, seen_at = [], []
        for j, c, _, _ in jobs:
            for r in range(rows):
                q = qg[j, c, r * vec:(r + 1) * vec, :]
                keys = kt[ids_s[j, c, 0, r]]
                scores.append(jnp.dot(q, keys, preferred_element_type=jnp.float32))
                seen_at.append(places < ids_s[j, c, 0, rows + r])
        scores = [
            jnp.where(visible, score * scale, masked_score)
            for score, visible in zip(scores, seen_at)
        ]
        peaks = [jnp.max(score, axis=1, keepdims=True) for score in scores]
        weights = [
            jnp.where(visible, jnp.exp(score - peak), 0.0)
            for score, visible, peak in zip(scores, seen_at, peaks)
        ]
        totals = [jnp.sum(weight, axis=1, keepdims=True) for weight in weights]
        mixes = []
        for n, (j, c, _, _) in enumerate(jobs):
            for r in range(rows):
                mixes.append(
                    jnp.dot(
                        weights[n * rows + r].astype(jnp.bfloat16),
                        vbuf[ids_s[j, c, 0, r]],
                        preferred_element_type=jnp.float32,
                    )
                )
        seen = [total > 0.0 for total in totals]
        safe = [jnp.where(some, total, 1.0) for some, total in zip(seen, totals)]
        lses = [
            jnp.where(some, peak + jnp.log(total), masked_score)
            for some, peak, total in zip(seen, peaks, safe)
        ]
        for n, (j, c, write, tiles) in enumerate(jobs):
            packed = tiles[...]
            for r in range(rows):
                at_row = n * rows + r
                write(slice(r * vec, (r + 1) * vec), mixes[at_row] * (1.0 / safe[at_row]))
                for s in range(STEPS):
                    packed = jnp.where(
                        lane8 == half * pairs + r * STEPS + s,
                        lses[at_row][s * GROUP:(s + 1) * GROUP, :],
                        packed,
                    )
            tiles[...] = packed

    def y_mix(i, j):
        return remote(
            ys.at[j - 1, pl.ds(2 * i, 2)], yr.at[ny - j - 1, pl.ds(2 * i, 2)],
            cm_send.at[i, j], cm_recv.at[i, ny - j], peer(j),
        )

    def y_lse(i, j):
        return remote(
            yst.at[j - 1, i], yrt.at[ny - j - 1, i],
            cl_send.at[i, j], cl_recv.at[i, ny - j], peer(j),
        )

    def z_dev(c):
        return at(y, column(c))

    def z_mix(c):
        return remote(zs.at[c], zr.at[c], zm_send.at[c], zm_recv.at[c], z_dev(c))

    def z_lse(c):
        return remote(zst.at[lax.div(c, 2)], zrt.at[c], zl_send.at[c], zl_recv.at[c], z_dev(c))

    def shares(lses):
        top = lses[0]
        for lse in lses[1:]:
            top = jnp.maximum(top, lse)
        terms = [jnp.exp(lse - top) for lse in lses]
        total = terms[0]
        for term in terms[1:]:
            total = total + term
        inverse = 1.0 / total
        return [term * inverse for term in terms], top + jnp.log(total)

    def blend(parts, share, k, lanes):
        result = None
        for load_part, factor, lane in zip(parts, share, lanes):
            lane = lane + 2 * k
            wide = jnp.concatenate(
                [
                    jnp.broadcast_to(factor[:, lane:lane + 1], (GROUP, HD)),
                    jnp.broadcast_to(factor[:, lane + 1:lane + 2], (GROUP, HD)),
                ],
                axis=0,
            )
            term = load_part(slice(16 * k, 16 * k + 16)).astype(jnp.float32) * wide
            result = term if result is None else result + term
        return result

    def stage_a(i):
        @pl.when(i > 0)
        def _():
            q_send(2 * i).wait_recv()
            id_send(2 * i).wait_recv()

        q_send(2 * i + 1).wait_recv()
        id_send(2 * i + 1).wait_recv()
        for j in range(1, ny):
            id_peer(i, j).start()
        for j in (1, 3):
            q_peer(i, j).start()

    def stage_relay(i):
        for j in (1, 3):
            q_peer(i, ny - j).wait_recv()
            q_relay(i, ny - j).start()

    def stage_ids(i):
        for j in range(1, ny):
            id_peer(i, ny - j).wait_recv()
        ids_local(i).start()

    def stage_b(i):
        ids_local(i).wait()
        for j in (1, 3):
            q_relay(i, j).wait_recv()

        @pl.loop(0, 2)
        def _(cc):
            c = 2 * i + cc

            def write(where, value):
                ya[c, where, :] = value

            def write_to(j):
                def write(where, value):
                    ys[j - 1, c, where, :] = value.astype(jnp.bfloat16)

                return write

            for first in range(0, ny, 4):
                jobs = [
                    (j, c, write if j == 0 else write_to(j), yl.at[i] if j == 0 else yst.at[j - 1, i])
                    for j in range(first, min(first + 4, ny))
                ]
                attend(jobs, cc)

        for j in range(1, ny):
            y_mix(i, j).start()
            y_lse(i, j).start()

    def stage_c(i):
        for j in range(1, ny):
            y_mix(i, ny - j).wait_recv()
            y_lse(i, ny - j).wait_recv()

        share, lse = shares([yl[i]] + [yrt[j - 1, i] for j in range(1, ny)])
        zst[i] = lse
        for cc in range(2):
            c = 2 * i + cc
            parts = [lambda where: ya[c, where, :]]
            for j in range(1, ny):
                parts.append(lambda where, j=j: yr[j - 1, c, where, :])
            for k in range(size // 16):
                zs[c, 16 * k:16 * k + 16, :] = blend(
                    parts, share, k, [cc * pairs] * ny
                ).astype(jnp.bfloat16)

            @pl.when(c > 0)
            def _():
                z_mix(c).start()
                z_lse(c).start()

    @pl.loop(0, steps + 4)
    def _(i):
        @pl.when(i < steps)
        def _():
            stage_a(i)

        @pl.when(i == 1)
        def _():
            ready()

        @pl.when(jnp.logical_and(i >= 1, i < steps + 1))
        def _():
            stage_relay(i - 1)
            stage_ids(i - 1)

        @pl.when(i >= 4)
        def _():
            stage_c(i - 4)

        @pl.when(jnp.logical_and(i >= 2, i < steps + 2))
        def _():
            stage_b(i - 2)

        @pl.when(i == steps + 2)
        def _():
            own_tokens()

    @pl.loop(1, nz)
    def _(c):
        z_mix(c).wait_recv()
        z_lse(c).wait_recv()

    parts = [lambda where: own_a[where, :], lambda where: zs[0, where, :]]
    lses = [own_l[:, 0:pairs], zst[0][:, 0:pairs]]
    for c in range(1, nz):
        parts.append(lambda where, c=c: zr[c, where, :])
        lses.append(zrt[c][:, c % 2 * pairs:(c % 2 + 1) * pairs])
    share, _ = shares(lses)
    for k in range(size // 16):
        ag[0, 0, 16 * k:16 * k + 16, :] = blend(parts, share, k, [0] * (nz + 1)).astype(jnp.bfloat16)

    def d_send_to(c):
        return remote(ag.at[0, 0], ag.at[0, c], d_send.at[c], d_recv.at[c], mirror(c))

    def d_peer(i, j):
        return remote(
            ag.at[0, pl.ds(2 * i, 2)], ag.at[ny - j, pl.ds(2 * i, 2)],
            dy_send.at[i, j], dy_recv.at[i, ny - j], peer(j),
        )

    for c in range(1, nz):
        d_send_to(c).start()

    def gather(i):
        @pl.when(i > 0)
        def _():
            d_send_to(2 * i).wait_recv()

        d_send_to(2 * i + 1).wait_recv()
        for j in range(1, ny):
            d_peer(i, j).start()

    blocks = ny * nz // nk

    def e_copy(owner):
        other = lax.div(owner, blocks)
        back = lax.rem(kv - other + nk, nk)
        return other != kv, remote(
            part.at[owner], er.at[back, lax.rem(owner, blocks)],
            e_send.at[owner], e_recv.at[back, lax.rem(owner, blocks)], (seq, other),
        )

    def project(i):
        for j in range(1, ny):
            d_peer(i, ny - j).wait_recv()
        for cc in range(2):
            for j in range(ny):
                first = (cc * ny + j) * size
                fs[first:first + size, :] = ag[j, 2 * i + cc].astype(jnp.float32)
        total = None
        for h in range(GROUP):
            piece = fs[pl.ds(h, 2 * ny * pairs, stride=GROUP), :].astype(jnp.bfloat16)
            term = jnp.dot(
                piece, wbuf[h * HD:(h + 1) * HD, :], preferred_element_type=jnp.float32
            )
            total = term if total is None else total + term
        ms[...] = total
        for cc in range(2):
            column = lax.rem((z - i if cc == 0 else z + i + 1) + nz, nz)
            for j in range(ny):
                owner = lax.rem(y + j, ny) * nz + column
                first = (cc * ny + j) * pairs
                part[owner] = ms[first:first + pairs, :]
                away, copy = e_copy(owner)

                @pl.when(away)
                def _(copy=copy):
                    copy.start()

    @pl.loop(0, steps + 1)
    def _(i):
        @pl.when(i < steps)
        def _():
            gather(i)

        @pl.when(i >= 1)
        def _():
            project(i - 1)

    for c in range(1, nk):
        for g in range(blocks):
            remote(
                part.at[g], er.at[c, g], e_send.at[g], e_recv.at[c, g],
                (seq, lax.rem(kv + c, nk)),
            ).wait_recv()
    result = part[pl.ds(kv * blocks, blocks)]
    for c in range(1, nk):
        result = result + er[c]
    for g in range(blocks):
        for r in range(rows):
            out_ref[g * rows + r] = result[g, r * STEPS:(r + 1) * STEPS, :].astype(out_ref.dtype)

    @pl.loop(0, steps)
    def _(i):
        for j in (1, 3):
            q_peer(i, j).wait_send()
            q_relay(i, j).wait_send()
        for j in range(1, ny):
            id_peer(i, j).wait_send()
            y_mix(i, j).wait_send()
            y_lse(i, j).wait_send()
            d_peer(i, j).wait_send()

    @pl.loop(1, nz)
    def _(c):
        q_send(c).wait_send()
        id_send(c).wait_send()
        z_mix(c).wait_send()
        z_lse(c).wait_send()
        d_send_to(c).wait_send()

    @pl.loop(0, ny * nz)
    def _(owner):
        away, copy = e_copy(owner)

        @pl.when(away)
        def _():
            copy.wait_send()


def solution(mesh, ny=None):
    nseq, nk = mesh.shape["seq"], mesh.shape["kvh"]
    ny = 4 if ny is None else ny
    nz = nseq // ny
    steps = nz // 2

    def shards(queries, new_keys, new_values, key_cache, value_cache, doc_ids, prefix_len, out_weight):
        rows = queries.shape[0]
        size = rows * STEPS * GROUP
        pairs = rows * STEPS
        blocks = nseq // nk
        bf, f32 = jnp.bfloat16, jnp.float32
        vmem = pl.BlockSpec(memory_space=pltpu.VMEM)
        anyw = pl.BlockSpec(memory_space=pl.ANY)
        dma = pltpu.SemaphoreType.DMA
        return pl.pallas_call(
            functools.partial(kernel, ny, nz, nk),
            out_shape=jax.ShapeDtypeStruct((blocks * rows, STEPS, HD), bf),
            in_specs=[anyw] * 8,
            out_specs=vmem,
            scratch_shapes=[
                pltpu.VMEM(queries.shape, bf),
                pltpu.VMEM(new_keys.shape, bf),
                pltpu.VMEM(new_values.shape, bf),
                pltpu.SMEM(doc_ids.shape, jnp.int32),
                pltpu.SMEM(prefix_len.shape, jnp.int32),
                pltpu.VMEM(key_cache.shape, bf),
                pltpu.VMEM((key_cache.shape[0], HD, key_cache.shape[1]), bf),
                pltpu.VMEM(value_cache.shape, bf),
                pltpu.VMEM(out_weight.shape, bf),
                pltpu.VMEM((size, HD), f32),
                pltpu.VMEM((ny, nz, size, HD), bf),
                pltpu.VMEM((ny, nz, 1, HD), jnp.int32),
                pltpu.SMEM((ny, nz, 1, HD), jnp.int32),
                pltpu.VMEM((size, HD), f32),
                pltpu.VMEM((GROUP, HD), f32),
                pltpu.VMEM((nz, size, HD), f32),
                pltpu.VMEM((steps, GROUP, HD), f32),
                pltpu.VMEM((ny - 1, nz, size, HD), bf),
                pltpu.VMEM((ny - 1, steps, GROUP, HD), f32),
                pltpu.VMEM((ny - 1, nz, size, HD), bf),
                pltpu.VMEM((ny - 1, steps, GROUP, HD), f32),
                pltpu.VMEM((nz, size, HD), bf),
                pltpu.VMEM((steps, GROUP, HD), f32),
                pltpu.VMEM((nz, size, HD), bf),
                pltpu.VMEM((nz, GROUP, HD), f32),
                pltpu.VMEM((ny, nz, size, HD), bf),
                pltpu.VMEM((2 * ny * size, HD), f32),
                pltpu.VMEM((2 * ny * pairs, HD), f32),
                pltpu.VMEM((nseq, pairs, HD), f32),
                pltpu.VMEM((nk, blocks, pairs, HD), f32),
                dma((8,)), dma((steps,)), dma((steps, ny)), dma((steps, ny)),
                dma((nz,)), dma((nz,)), dma((nz,)), dma((nz,)),
                dma((steps, ny)), dma((steps, ny)), dma((steps, ny)), dma((steps, ny)),
                dma((steps, ny)), dma((steps, ny)), dma((steps, ny)), dma((steps, ny)),
                dma((nz,)), dma((nz,)), dma((nz,)), dma((nz,)),
                dma((nz,)), dma((nz,)), dma((steps, ny)), dma((steps, ny)),
                dma((nseq,)), dma((nk, blocks)),
            ],
            compiler_params=pltpu.CompilerParams(
                collective_id=0, has_side_effects=True, vmem_limit_bytes=60 * 1024 * 1024
            ),
        )(queries, new_keys, new_values, doc_ids, prefix_len, key_cache, value_cache, out_weight)

    return jax.shard_map(
        shards,
        mesh=mesh,
        in_specs=(
            P("seq", None, "kvh"),
            P("seq", None, "kvh"),
            P("seq", None, "kvh"),
            P(None, "seq", "kvh"),
            P(None, "seq", "kvh"),
            P("seq"),
            P("seq"),
            P("kvh", "seq"),
        ),
        out_specs=P("kvh", None, "seq"),
        check_vma=False,
    )
```

```python
import functools
import math

import jax
import jax.numpy as jnp
from jax import lax
from jax.experimental import pallas as pl
from jax.experimental.pallas import tpu as pltpu
from jax.sharding import PartitionSpec as P

HD = 128
STEPS = 4
GROUP = 8
MESH = pl.DeviceIdType.MESH
masked_score = -1e30


def kernel(
    ny, nz, nk,
    q_hbm, nk_hbm, nv_hbm, doc_hbm, len_hbm, k_hbm, v_hbm, w_hbm,
    out_ref,
    q_ref, nk_ref, nv_ref, doc_ref, len_ref, kbuf, kt, vbuf, wbuf, qf, qg, idg, ids_s, own_a, own_l,
    ya, yl, ys, yst, yr, yrt, zs, zst, zr, zrt, ag, fs, ms, part, er,
    load_sem, ids_sem, iy_send, iy_recv,
    a_send, a_recv, i_send, i_recv, ay_send, ay_recv, ar_send, ar_recv,
    cm_send, cm_recv, cl_send, cl_recv, zm_send, zm_recv, zl_send, zl_recv,
    d_send, d_recv, dy_send, dy_recv, e_send, e_recv,
):
    seq, kv = lax.axis_index("seq"), lax.axis_index("kvh")
    y, z = lax.div(seq, nz), lax.rem(seq, nz)
    rows = q_ref.shape[0]
    vec = STEPS * GROUP
    pairs = rows * STEPS
    size = rows * vec
    steps = nz // 2
    tok = k_hbm.shape[1]
    scale = 1.0 / math.sqrt(HD)

    def at(yy, zz):
        return (lax.rem(yy + ny, ny) * nz + lax.rem(zz + nz, nz), kv)

    def peer(j):
        return at(y + j, z)

    def remote(src, dst, ssem, rsem, dev):
        return pltpu.make_async_remote_copy(
            src_ref=src, dst_ref=dst, send_sem=ssem, recv_sem=rsem,
            device_id=dev, device_id_type=MESH,
        )

    def landed(ref, sem):
        pltpu.make_async_copy(ref, ref, sem).wait()

    barrier = pltpu.get_barrier_semaphore()
    for j in range(1, ny):
        pl.semaphore_signal(barrier, inc=1, device_id=peer(j), device_id_type=MESH)
    for c in range(1, nz):
        pl.semaphore_signal(barrier, inc=1, device_id=at(y, z + c), device_id_type=MESH)
    for c in range(1, nk):
        pl.semaphore_signal(
            barrier, inc=1, device_id=(seq, lax.rem(kv + c, nk)), device_id_type=MESH
        )

    loads = [
        pltpu.make_async_copy(src, dst, load_sem.at[n])
        for n, (src, dst) in enumerate([
            (q_hbm, q_ref), (doc_hbm, doc_ref), (len_hbm, len_ref), (nk_hbm, nk_ref),
            (nv_hbm, nv_ref), (k_hbm, kbuf), (v_hbm, vbuf), (w_hbm, wbuf),
        ])
    ]
    for load in loads:
        load.start()
    for load in loads[:3]:
        load.wait()

    for r in range(rows):
        for h in range(GROUP):
            qf[pl.ds(r * vec + h, STEPS, stride=GROUP), :] = q_ref[
                r, :, h * HD:(h + 1) * HD
            ].astype(jnp.float32)
    qg[0, 0] = qf[...].astype(jnp.bfloat16)
    lane1 = lax.broadcasted_iota(jnp.int32, (1, HD), 1)
    own_ids = jnp.zeros((1, HD), jnp.int32)
    for r in range(rows):
        own_ids = jnp.where(lane1 == r, doc_ref[r], own_ids)
        own_ids = jnp.where(lane1 == rows + r, len_ref[r], own_ids)
    idg[0, 0] = own_ids

    pl.semaphore_wait(barrier, (ny - 1) + (nz - 1) + (nk - 1))

    def column(c):
        i = lax.div(c, 2)
        return jnp.where(lax.rem(c, 2) == 0, z - i, z + i + 1)

    def mirror(c):
        i = lax.div(c, 2)
        return at(y, jnp.where(lax.rem(c, 2) == 0, z + i, z - i - 1))

    def q_send(c):
        return remote(qg.at[0, 0], qg.at[0, c], a_send.at[0], a_recv.at[c // 2], mirror(c))

    def id_send(c):
        return remote(idg.at[0, 0], idg.at[0, c], i_send.at[0], i_recv.at[c // 2], mirror(c))

    def id_peer(i, j):
        return remote(
            idg.at[0, pl.ds(2 * i, 2)], idg.at[ny - j, pl.ds(2 * i, 2)],
            iy_send.at[0], iy_recv.at[i], peer(j),
        )

    def q_peer(i, j):
        return remote(
            qg.at[0, pl.ds(2 * i, 2)], qg.at[ny - j, pl.ds(2 * i, 2)],
            ay_send.at[0], ay_recv.at[i], peer(j),
        )

    def q_relay(i, j):
        c = 2 * i + (j - 1) // 2
        return remote(
            qg.at[ny - j, c], qg.at[2, c], ar_send.at[0], ar_recv.at[i], peer(j)
        )

    def ids_local(i):
        return pltpu.make_async_copy(
            idg.at[:, pl.ds(2 * i, 2)], ids_s.at[:, pl.ds(2 * i, 2)], ids_sem.at[i]
        )

    for c in range(1, nz):
        id_send(c).start()
    for c in range(1, nz):
        q_send(c).start()

    lane8 = lax.broadcasted_iota(jnp.int32, (GROUP, HD), 1)

    def own_tokens():
        loads[3].wait()
        loads[4].wait()
        step_of = lax.broadcasted_iota(jnp.int32, (vec, 1), 0) // GROUP
        stats = jnp.full((GROUP, HD), masked_score, jnp.float32)
        for r in range(rows):
            q = qf[r * vec:(r + 1) * vec, :]
            keys = nk_ref[r].astype(jnp.float32)
            values = nv_ref[r].astype(jnp.float32)
            scores = []
            for t in range(STEPS):
                score = jnp.sum(q * keys[t:t + 1, :], axis=1, keepdims=True) * scale
                scores.append(jnp.where(step_of >= t, score, masked_score))
            peak = scores[0]
            for t in range(1, STEPS):
                peak = jnp.maximum(peak, scores[t])
            total = jnp.zeros((vec, 1), jnp.float32)
            mix = jnp.zeros((vec, HD), jnp.float32)
            for t in range(STEPS):
                weight = jnp.where(step_of >= t, jnp.exp(scores[t] - peak), 0.0)
                total = total + weight
                mix = mix + weight.astype(jnp.bfloat16).astype(jnp.float32) * values[t:t + 1, :]
            own_a[r * vec:(r + 1) * vec, :] = mix / total
            lse = peak + jnp.log(total)
            for s in range(STEPS):
                stats = jnp.where(
                    lane8 == r * STEPS + s, lse[s * GROUP:(s + 1) * GROUP, :], stats
                )
        own_l[...] = stats

    def ready():
        for load in loads[5:]:
            load.wait()

        for d in range(kbuf.shape[0]):
            kt[d] = kbuf[d].T

        yl[...] = jnp.full(yl.shape, masked_score, jnp.float32)
        yst[...] = jnp.full(yst.shape, masked_score, jnp.float32)

    places = seq * tok + lax.broadcasted_iota(jnp.int32, (1, tok), 1)

    def attend(jobs, half):
        scores, seen_at = [], []
        for j, c, _, _ in jobs:
            for r in range(rows):
                q = qg[j, c, r * vec:(r + 1) * vec, :]
                keys = kt[ids_s[j, c, 0, r]]
                scores.append(jnp.dot(q, keys, preferred_element_type=jnp.float32))
                seen_at.append(places < ids_s[j, c, 0, rows + r])
        scores = [
            jnp.where(visible, score * scale, masked_score)
            for score, visible in zip(scores, seen_at)
        ]
        peaks = [jnp.max(score, axis=1, keepdims=True) for score in scores]
        weights = [
            jnp.where(visible, jnp.exp(score - peak), 0.0)
            for score, visible, peak in zip(scores, seen_at, peaks)
        ]
        totals = [jnp.sum(weight, axis=1, keepdims=True) for weight in weights]
        mixes = []
        for n, (j, c, _, _) in enumerate(jobs):
            for r in range(rows):
                mixes.append(
                    jnp.dot(
                        weights[n * rows + r].astype(jnp.bfloat16),
                        vbuf[ids_s[j, c, 0, r]],
                        preferred_element_type=jnp.float32,
                    )
                )
        seen = [total > 0.0 for total in totals]
        safe = [jnp.where(some, total, 1.0) for some, total in zip(seen, totals)]
        lses = [
            jnp.where(some, peak + jnp.log(total), masked_score)
            for some, peak, total in zip(seen, peaks, safe)
        ]
        for n, (j, c, write, tiles) in enumerate(jobs):
            packed = tiles[...]
            for r in range(rows):
                at_row = n * rows + r
                write(slice(r * vec, (r + 1) * vec), mixes[at_row] * (1.0 / safe[at_row]))
                for s in range(STEPS):
                    packed = jnp.where(
                        lane8 == half * pairs + r * STEPS + s,
                        lses[at_row][s * GROUP:(s + 1) * GROUP, :],
                        packed,
                    )
            tiles[...] = packed

    def y_mix(i, j):
        return remote(
            ys.at[j - 1, pl.ds(2 * i, 2)], yr.at[ny - j - 1, pl.ds(2 * i, 2)],
            cm_send.at[0], cm_recv.at[i], peer(j),
        )

    def y_lse(i, j):
        return remote(
            yst.at[j - 1, i], yrt.at[ny - j - 1, i],
            cl_send.at[0], cl_recv.at[i], peer(j),
        )

    def z_dev(c):
        return at(y, column(c))

    def z_mix(c):
        return remote(zs.at[c], zr.at[c], zm_send.at[0], zm_recv.at[0], z_dev(c))

    def z_lse(c):
        return remote(zst.at[lax.div(c, 2)], zrt.at[c], zl_send.at[0], zl_recv.at[0], z_dev(c))

    def shares(lses):
        top = lses[0]
        for lse in lses[1:]:
            top = jnp.maximum(top, lse)
        terms = [jnp.exp(lse - top) for lse in lses]
        total = terms[0]
        for term in terms[1:]:
            total = total + term
        inverse = 1.0 / total
        return [term * inverse for term in terms], top + jnp.log(total)

    def blend(parts, share, k, lanes):
        result = None
        for load_part, factor, lane in zip(parts, share, lanes):
            lane = lane + 2 * k
            wide = jnp.concatenate(
                [
                    jnp.broadcast_to(factor[:, lane:lane + 1], (GROUP, HD)),
                    jnp.broadcast_to(factor[:, lane + 1:lane + 2], (GROUP, HD)),
                ],
                axis=0,
            )
            term = load_part(slice(16 * k, 16 * k + 16)).astype(jnp.float32) * wide
            result = term if result is None else result + term
        return result

    def stage_a(i):
        @pl.when(i > 0)
        def _():
            landed(qg.at[0, pl.ds(2 * i, 2)], a_recv.at[i])
            landed(idg.at[0, pl.ds(2 * i, 2)], i_recv.at[i])

        @pl.when(i == 0)
        def _():
            landed(qg.at[0, 1], a_recv.at[0])
            landed(idg.at[0, 1], i_recv.at[0])

        for j in range(1, ny):
            id_peer(i, j).start()
        for j in (1, 3):
            q_peer(i, j).start()

    def stage_relay(i):
        landed(qg.at[pl.ds(0, 2), pl.ds(2 * i, 2)], ay_recv.at[i])
        for j in (1, 3):
            q_relay(i, j).start()

    def stage_ids(i):
        landed(idg.at[pl.ds(1, ny - 1), pl.ds(2 * i, 2)], iy_recv.at[i])
        ids_local(i).start()

    def stage_b(i):
        ids_local(i).wait()
        landed(qg.at[2, pl.ds(2 * i, 2)], ar_recv.at[i])

        @pl.loop(0, 2)
        def _(cc):
            c = 2 * i + cc

            def write(where, value):
                ya[c, where, :] = value

            def write_to(j):
                def write(where, value):
                    ys[j - 1, c, where, :] = value.astype(jnp.bfloat16)

                return write

            for first in range(0, ny, 4):
                jobs = [
                    (j, c, write if j == 0 else write_to(j), yl.at[i] if j == 0 else yst.at[j - 1, i])
                    for j in range(first, min(first + 4, ny))
                ]
                attend(jobs, cc)

        for j in range(1, ny):
            y_mix(i, j).start()
            y_lse(i, j).start()

    def stage_c(i):
        landed(yr.at[:, pl.ds(2 * i, 2)], cm_recv.at[i])
        landed(yrt.at[:, i], cl_recv.at[i])

        share, lse = shares([yl[i]] + [yrt[j - 1, i] for j in range(1, ny)])
        zst[i] = lse
        for cc in range(2):
            c = 2 * i + cc
            parts = [lambda where: ya[c, where, :]]
            for j in range(1, ny):
                parts.append(lambda where, j=j: yr[j - 1, c, where, :])
            for k in range(size // 16):
                zs[c, 16 * k:16 * k + 16, :] = blend(
                    parts, share, k, [cc * pairs] * ny
                ).astype(jnp.bfloat16)

            @pl.when(c > 0)
            def _():
                z_mix(c).start()
                z_lse(c).start()

    @pl.loop(0, steps + 4)
    def _(i):
        @pl.when(i < steps)
        def _():
            stage_a(i)

        @pl.when(i == 1)
        def _():
            ready()

        @pl.when(jnp.logical_and(i >= 1, i < steps + 1))
        def _():
            stage_relay(i - 1)
            stage_ids(i - 1)

        @pl.when(i >= 4)
        def _():
            stage_c(i - 4)

        @pl.when(jnp.logical_and(i >= 2, i < steps + 2))
        def _():
            stage_b(i - 2)

        @pl.when(i == steps + 2)
        def _():
            own_tokens()

    landed(zr.at[pl.ds(1, nz - 1)], zm_recv.at[0])
    landed(zrt.at[pl.ds(1, nz - 1)], zl_recv.at[0])

    parts = [lambda where: own_a[where, :], lambda where: zs[0, where, :]]
    lses = [own_l[:, 0:pairs], zst[0][:, 0:pairs]]
    for c in range(1, nz):
        parts.append(lambda where, c=c: zr[c, where, :])
        lses.append(zrt[c][:, c % 2 * pairs:(c % 2 + 1) * pairs])
    share, _ = shares(lses)
    for k in range(size // 16):
        ag[0, 0, 16 * k:16 * k + 16, :] = blend(parts, share, k, [0] * (nz + 1)).astype(jnp.bfloat16)

    def d_send_to(c):
        return remote(ag.at[0, 0], ag.at[0, c], d_send.at[0], d_recv.at[c // 2], mirror(c))

    def d_peer(i, j):
        return remote(
            ag.at[0, pl.ds(2 * i, 2)], ag.at[ny - j, pl.ds(2 * i, 2)],
            dy_send.at[0], dy_recv.at[i], peer(j),
        )

    for c in range(1, nz):
        d_send_to(c).start()

    def gather(i):
        @pl.when(i > 0)
        def _():
            landed(ag.at[0, pl.ds(2 * i, 2)], d_recv.at[i])

        @pl.when(i == 0)
        def _():
            landed(ag.at[0, 1], d_recv.at[0])

        for j in range(1, ny):
            d_peer(i, j).start()

    blocks = ny * nz // nk

    def e_copy(owner):
        other = lax.div(owner, blocks)
        back = lax.rem(kv - other + nk, nk)
        return other != kv, remote(
            part.at[owner], er.at[back, lax.rem(owner, blocks)],
            e_send.at[0], e_recv.at[back], (seq, other),
        )

    def project(i):
        landed(ag.at[pl.ds(1, ny - 1), pl.ds(2 * i, 2)], dy_recv.at[i])
        for cc in range(2):
            for j in range(ny):
                first = (cc * ny + j) * size
                fs[first:first + size, :] = ag[j, 2 * i + cc].astype(jnp.float32)
        total = None
        for h in range(GROUP):
            piece = fs[pl.ds(h, 2 * ny * pairs, stride=GROUP), :].astype(jnp.bfloat16)
            term = jnp.dot(
                piece, wbuf[h * HD:(h + 1) * HD, :], preferred_element_type=jnp.float32
            )
            total = term if total is None else total + term
        ms[...] = total
        for cc in range(2):
            column = lax.rem((z - i if cc == 0 else z + i + 1) + nz, nz)
            for j in range(ny):
                owner = lax.rem(y + j, ny) * nz + column
                first = (cc * ny + j) * pairs
                part[owner] = ms[first:first + pairs, :]
                away, copy = e_copy(owner)

                @pl.when(away)
                def _(copy=copy):
                    copy.start()

    def sent():
        landed(qg.at[0, pl.ds(1, nz - 1)], a_send.at[0])
        landed(idg.at[0, pl.ds(1, nz - 1)], i_send.at[0])
        landed(qg.at[pl.ds(0, 2)], ay_send.at[0])
        landed(qg.at[0], ar_send.at[0])
        landed(idg.at[pl.ds(1, ny - 1)], iy_send.at[0])
        landed(ys, cm_send.at[0])
        landed(yst, cl_send.at[0])
        landed(zr.at[pl.ds(1, nz - 1)], zm_send.at[0])
        landed(zrt.at[pl.ds(1, nz - 1)], zl_send.at[0])

    @pl.loop(0, steps + 1)
    def _(i):
        @pl.when(i < steps)
        def _():
            gather(i)

        @pl.when(i == 0)
        def _():
            sent()

        @pl.when(i >= 1)
        def _():
            project(i - 1)

    landed(ag.at[0, pl.ds(1, nz - 1)], d_send.at[0])
    landed(ag.at[pl.ds(1, ny - 1)], dy_send.at[0])

    for c in range(1, nk):
        landed(er.at[c], e_recv.at[c])
    result = part[pl.ds(kv * blocks, blocks)]
    for c in range(1, nk):
        result = result + er[c]
    for g in range(blocks):
        for r in range(rows):
            out_ref[g * rows + r] = result[g, r * STEPS:(r + 1) * STEPS, :].astype(out_ref.dtype)

    landed(part.at[pl.ds(0, (nk - 1) * blocks)], e_send.at[0])


def solution(mesh, ny=None):
    nseq, nk = mesh.shape["seq"], mesh.shape["kvh"]
    ny = 4 if ny is None else ny
    nz = nseq // ny
    steps = nz // 2

    def shards(queries, new_keys, new_values, key_cache, value_cache, doc_ids, prefix_len, out_weight):
        rows = queries.shape[0]
        size = rows * STEPS * GROUP
        pairs = rows * STEPS
        blocks = nseq // nk
        bf, f32 = jnp.bfloat16, jnp.float32
        vmem = pl.BlockSpec(memory_space=pltpu.VMEM)
        anyw = pl.BlockSpec(memory_space=pl.ANY)
        dma = pltpu.SemaphoreType.DMA
        return pl.pallas_call(
            functools.partial(kernel, ny, nz, nk),
            out_shape=jax.ShapeDtypeStruct((blocks * rows, STEPS, HD), bf),
            in_specs=[anyw] * 8,
            out_specs=vmem,
            scratch_shapes=[
                pltpu.VMEM(queries.shape, bf),
                pltpu.VMEM(new_keys.shape, bf),
                pltpu.VMEM(new_values.shape, bf),
                pltpu.SMEM(doc_ids.shape, jnp.int32),
                pltpu.SMEM(prefix_len.shape, jnp.int32),
                pltpu.VMEM(key_cache.shape, bf),
                pltpu.VMEM((key_cache.shape[0], HD, key_cache.shape[1]), bf),
                pltpu.VMEM(value_cache.shape, bf),
                pltpu.VMEM(out_weight.shape, bf),
                pltpu.VMEM((size, HD), f32),
                pltpu.VMEM((ny, nz, size, HD), bf),
                pltpu.VMEM((ny, nz, 1, HD), jnp.int32),
                pltpu.SMEM((ny, nz, 1, HD), jnp.int32),
                pltpu.VMEM((size, HD), f32),
                pltpu.VMEM((GROUP, HD), f32),
                pltpu.VMEM((nz, size, HD), f32),
                pltpu.VMEM((steps, GROUP, HD), f32),
                pltpu.VMEM((ny - 1, nz, size, HD), bf),
                pltpu.VMEM((ny - 1, steps, GROUP, HD), f32),
                pltpu.VMEM((ny - 1, nz, size, HD), bf),
                pltpu.VMEM((ny - 1, steps, GROUP, HD), f32),
                pltpu.VMEM((nz, size, HD), bf),
                pltpu.VMEM((steps, GROUP, HD), f32),
                pltpu.VMEM((nz, size, HD), bf),
                pltpu.VMEM((nz, GROUP, HD), f32),
                pltpu.VMEM((ny, nz, size, HD), bf),
                pltpu.VMEM((2 * ny * size, HD), f32),
                pltpu.VMEM((2 * ny * pairs, HD), f32),
                pltpu.VMEM((nseq, pairs, HD), f32),
                pltpu.VMEM((nk, blocks, pairs, HD), f32),
                dma((8,)), dma((steps,)), dma((1,)), dma((steps,)),
                dma((1,)), dma((steps,)), dma((1,)), dma((steps,)),
                dma((1,)), dma((steps,)), dma((1,)), dma((steps,)),
                dma((1,)), dma((steps,)), dma((1,)), dma((steps,)),
                dma((1,)), dma((1,)), dma((1,)), dma((1,)),
                dma((1,)), dma((steps,)), dma((1,)), dma((steps,)),
                dma((1,)), dma((nk,)),
            ],
            compiler_params=pltpu.CompilerParams(
                collective_id=0, has_side_effects=True, vmem_limit_bytes=60 * 1024 * 1024
            ),
        )(queries, new_keys, new_values, doc_ids, prefix_len, key_cache, value_cache, out_weight)

    return jax.shard_map(
        shards,
        mesh=mesh,
        in_specs=(
            P("seq", None, "kvh"),
            P("seq", None, "kvh"),
            P("seq", None, "kvh"),
            P(None, "seq", "kvh"),
            P(None, "seq", "kvh"),
            P("seq"),
            P("seq"),
            P("kvh", "seq"),
        ),
        out_specs=P("kvh", None, "seq"),
        check_vma=False,
    )
```
